32 devices in a mesh: shot: 4 (over x, core), rcv: 8 (over z, y).
Axes of the slice: x: 2, y: 2, z: 4, core: 2. Of those that a mesh axis runs over, the one named last changes fastest.
Arguments:
- data: float32 [1, 2, 8192, 1024], P(None, None, 'rcv', 'shot'), may hold values from -6 to 6
- impulse: float32 [1, 2, 8192, 8192], P(None, None, 'rcv'), may hold values from -0.0625 to 0.0625
- wavelet: float32 [1, 2], replicated, may hold values from -96 to 96
- live: int32 [8192, 1024], P('rcv', 'shot'), may hold values from 0 to 1, as said below
Outputs:
- residual: float32 [1, 2, 8192, 1024], P(None, None, 'rcv', 'shot')
- gradient: float32 [1, 2, 8192, 8192], P(None, None, 'rcv', 'shot')
The draws below stay inside these ranges and needn't reach their ends.
Inputs may be any that keep to these rules, and one draw needn't show every extreme that they name: live[r, s] is 0 where |r - s * 8| is at most a per-shot half gap of 1 to 4 positions, and at scattered dead traces; 1 elsewhere.
All inputs are finite; a program needn't handle non-finite values.
Results may differ from the reference program's by a relative error of at most 0.000084.
Values sent between devices are 32-bit elements; how exact they have to be, the bound alone decides.
A program may use at most 320 MiB of HBM per device.

```python
import jax
import jax.numpy as jnp
from jax import lax

NR = 8192
FREQS = 1
NS = 1024


def draw_live(key, part):
    key_gap, key_dead = jax.random.split(jax.random.fold_in(key, 7))
    rows = lax.broadcasted_iota(jnp.int32, (NR, NS), 0)
    cols = lax.broadcasted_iota(jnp.int32, (NR, NS), 1)
    centre = cols * (NR // NS)
    gaps = jax.random.randint(key_gap, (1, NS), 1, 5)
    near = jnp.abs(rows - centre) <= gaps
    dead = jax.random.randint(key_dead, (NR, NS), 0, 25) == 0
    return jnp.where(near | dead, 0, 1).astype(jnp.int32)


def steps_of(key, dims, cuts, least, largest):
    loudness, own = 1.0, jax.random.fold_in(key, 6)
    for axis_at, blocks in cuts:
        draws = jnp.exp(jax.random.uniform(jax.random.fold_in(own, axis_at), (blocks,), jnp.float32, least / len(cuts), largest / len(cuts)))
        loudness = loudness * jnp.repeat(draws, dims[axis_at] // blocks).reshape([-1 if axis == axis_at else 1 for axis in range(len(dims))])
    return loudness


def normal_values(rng, dims, deviation, reach, pieces=(), dtype=jnp.bfloat16):
    loudness = steps_of(rng, dims, pieces, -0.22, 0.18) if pieces else 1.0
    result = jax.random.normal(rng, dims, jnp.float32) * deviation * loudness
    return jnp.minimum(jnp.maximum(result, -reach), reach).astype(dtype)


def setup_inputs(seed: int = 0) -> dict:
    key_list = jax.random.split(jax.random.key(seed), 5)
    data = normal_values(key_list[0], (FREQS, 2, NR, NS), 1.0, 6.0, ((2, 8), (3, 4)), jnp.float32)
    impulse = normal_values(key_list[1], (FREQS, 2, NR, NR), NR ** -0.5, 0.0625, ((2, 8),), jnp.float32)
    wavelet = normal_values(key_list[2], (FREQS, 2), 16.0, 96.0, (), jnp.float32)
    live = draw_live(jax.random.fold_in(key_list[4], 71), 0)
    return dict(data=data, impulse=impulse, wavelet=wavelet, live=live)


def product(left, right, form):
    return jnp.einsum(form, left, right, precision=lax.Precision.HIGHEST, preferred_element_type=jnp.float32)


def reference(data, impulse, wavelet, live):
    mask = live.astype(jnp.float32)
    observed = data * mask[None, None]
    rows = lax.broadcasted_iota(jnp.int32, (NR, NS), 0)
    cols = lax.broadcasted_iota(jnp.int32, (NR, NS), 1)
    source = (rows == cols * (NR // NS)).astype(jnp.float32)
    panel_re = wavelet[:, 0][:, None, None] * source[None] - observed[:, 0]
    panel_im = wavelet[:, 1][:, None, None] * source[None] - observed[:, 1]
    imp_re = impulse[:, 0]
    imp_im = impulse[:, 1]
    pred_re = product(imp_re, panel_re, "frk,fks->frs") - product(imp_im, panel_im, "frk,fks->frs")
    pred_im = product(imp_re, panel_im, "frk,fks->frs") + product(imp_im, panel_re, "frk,fks->frs")
    res_re = mask[None] * (observed[:, 0] - pred_re)
    res_im = mask[None] * (observed[:, 1] - pred_im)
    residual = jnp.stack([res_re, res_im], axis=1)
    scale = -(NS ** -0.5)
    grad_re = product(res_re, panel_re, "frs,fks->frk") + product(res_im, panel_im, "frs,fks->frk")
    grad_im = product(res_im, panel_re, "frs,fks->frk") - product(res_re, panel_im, "frs,fks->frk")
    gradient = jnp.stack([grad_re, grad_im], axis=1) * scale
    return (residual, gradient)
```

```python
import functools

import jax
import jax.numpy as jnp
from jax import lax
from jax.experimental import pallas as pl
from jax.experimental.pallas import tpu as pltpu
from jax.sharding import PartitionSpec as P

MESH = pl.DeviceIdType.MESH
PRECISION = lax.Precision.HIGH


def product(left, right, form):
    return jnp.einsum(form, left, right, precision=PRECISION, preferred_element_type=jnp.float32)


def convolve(imp, panel):
    form = "rk,ks->rs"
    out_re = product(imp[0], panel[0], form) - product(imp[1], panel[1], form)
    out_im = product(imp[0], panel[1], form) + product(imp[1], panel[0], form)
    return jnp.stack([out_re, out_im])


def correlate(res, panel, scale):
    form = "rs,ks->rk"
    out_re = product(res[0], panel[0], form) + product(res[1], panel[1], form)
    out_im = product(res[1], panel[0], form) - product(res[0], panel[1], form)
    return jnp.stack([out_re, out_im]) * scale


def spread_kernel(planes, panel_ref, gath_ref, line_recv, y_recv, send_src, send_up, send_down, send_y, local_sem):
    j = lax.axis_index("shot")
    b = lax.axis_index("rcv")
    z, y = b // 2, lax.rem(b, 2)
    other = z * 2 + 1 - y
    rows, shots = panel_ref.shape[1], panel_ref.shape[2]

    barrier = pltpu.get_barrier_semaphore()
    for d in range(1, planes):
        pl.semaphore_signal(barrier, inc=1, device_id=(lax.rem(j + d, planes), b), device_id_type=MESH)
    pl.semaphore_signal(barrier, inc=1, device_id=(j, other), device_id_type=MESH)

    @pl.when(z < planes - 1)
    def _():
        pl.semaphore_signal(barrier, inc=1, device_id=(j, b + 2), device_id_type=MESH)

    @pl.when(z > 0)
    def _():
        pl.semaphore_signal(barrier, inc=1, device_id=(j, b - 2), device_id_type=MESH)

    ends = (z == 0).astype(jnp.int32) + (z == planes - 1).astype(jnp.int32)
    pl.semaphore_wait(barrier, planes + 2 - ends)

    def slot(a, side, p):
        return gath_ref.at[p, pl.ds(pl.multiple_of(side * rows, rows), rows), pl.ds(pl.multiple_of(a * shots, shots), shots)]

    def source(p):
        i = lax.rem(j - z + planes, planes)
        return pltpu.make_async_remote_copy(
            src_ref=panel_ref.at[p], dst_ref=slot(j, y, p), send_sem=send_src.at[p],
            recv_sem=line_recv.at[i * 2 + p], device_id=(z, b), device_id_type=MESH)

    def own(p):
        return pltpu.make_async_copy(panel_ref.at[p], slot(j, y, p), local_sem.at[p])

    @pl.when(j != z)
    def _():
        for p in range(2):
            source(p).start()

    @pl.when(j == z)
    def _():
        for p in range(2):
            own(p).start()

    def step(i, p):
        a = lax.rem(j + i, planes)
        ref = slot(a, y, p)
        n = i * 2 + p

        def to(dev, send, recv):
            return pltpu.make_async_remote_copy(
                src_ref=ref, dst_ref=ref, send_sem=send.at[n], recv_sem=recv.at[n],
                device_id=(j, dev), device_id_type=MESH)

        return n, to

    up_ok = jnp.logical_and(z >= j, z < planes - 1)
    down_ok = jnp.logical_and(z <= j, z > 0)
    for i in range(planes):
        for p in range(2):
            n, to = step(i, p)
            if i == 0:
                @pl.when(j == z)
                def _():
                    own(p).wait()

                @pl.when(j != z)
                def _():
                    to(other, send_y, line_recv).wait_recv()
            else:
                to(other, send_y, line_recv).wait_recv()

            @pl.when(up_ok)
            def _():
                to(b + 2, send_up, line_recv).start()

            @pl.when(down_ok)
            def _():
                to(b - 2, send_down, line_recv).start()

            to(other, send_y, y_recv).start()

    for i in range(planes):
        for p in range(2):
            n, to = step(i, p)

            @pl.when(up_ok)
            def _():
                to(b + 2, send_up, line_recv).wait_send()

            @pl.when(down_ok)
            def _():
                to(b - 2, send_down, line_recv).wait_send()

            to(other, send_y, y_recv).wait_send()
            a = lax.rem(j + i, planes)
            ref = slot(a, 1 - y, p)
            pltpu.make_async_remote_copy(
                src_ref=ref, dst_ref=ref, send_sem=send_y.at[n], recv_sem=y_recv.at[n],
                device_id=(j, other), device_id_type=MESH).wait_recv()

    @pl.when(j != z)
    def _():
        for p in range(2):
            source(p).wait_send()


def spread(panel, planes):
    _, rows, shots = panel.shape
    dma = pltpu.SemaphoreType.DMA
    return pl.pallas_call(
        functools.partial(spread_kernel, planes),
        out_shape=jax.ShapeDtypeStruct((2, 2 * rows, planes * shots), jnp.float32),
        in_specs=[pl.BlockSpec(memory_space=pl.ANY)],
        out_specs=pl.BlockSpec(memory_space=pl.ANY),
        scratch_shapes=[dma((2 * planes,)), dma((2 * planes,)), dma((2,)), dma((2 * planes,)),
                        dma((2 * planes,)), dma((2 * planes,)), dma((2,))],
        compiler_params=pltpu.CompilerParams(collective_id=0, has_side_effects=True),
    )(panel)


def local(data, impulse, wavelet, live):
    rows_dev = data.shape[2]
    shots_dev = data.shape[3]
    positions = impulse.shape[3]
    groups = lax.axis_size("shot")
    total_shots = shots_dev * groups
    spacing = positions // total_shots
    scale = -(total_shots ** (-0.5))
    j = lax.axis_index("shot")
    mask = live.astype(jnp.float32)
    observed = data[0] * mask[None]
    row_ids = lax.axis_index("rcv") * rows_dev + lax.broadcasted_iota(jnp.int32, (rows_dev, shots_dev), 0)
    col_ids = j * shots_dev + lax.broadcasted_iota(jnp.int32, (rows_dev, shots_dev), 1)
    source = (row_ids == col_ids * spacing).astype(jnp.float32)
    panel = wavelet[0][:, None, None] * source[None] - observed
    if lax.axis_size("rcv") == 2 * groups:
        part = spread(panel, groups)
    else:
        whole = lax.all_gather(panel, "rcv", axis=1, tiled=True)
        part = lax.all_to_all(whole, "shot", split_axis=1, concat_axis=2, tiled=True)
    quarter = positions // groups
    imp = lax.dynamic_slice_in_dim(impulse[0], j * quarter, quarter, axis=2)
    predicted = lax.psum_scatter(convolve(imp, part), "shot", scatter_dimension=2, tiled=True)
    residual = mask[None] * (observed - predicted)
    every = lax.all_gather(residual, "shot", axis=2, tiled=True)
    gradient = correlate(every, part, scale)
    return (residual[None], gradient[None])


def solution(mesh):
    placed = (P(None, None, "rcv", "shot"), P(None, None, "rcv", None), P(), P("rcv", "shot"))
    return jax.shard_map(
        local,
        mesh=mesh,
        in_specs=placed,
        out_specs=(P(None, None, "rcv", "shot"), P(None, None, "rcv", "shot")),
        check_vma=False,
    )
```

```python
import functools

import jax
import jax.numpy as jnp
from jax import lax
from jax.experimental import pallas as pl
from jax.experimental.pallas import tpu as pltpu
from jax.sharding import PartitionSpec as P

MESH = pl.DeviceIdType.MESH
PRECISION = lax.Precision.HIGH


def product(left, right, form):
    return jnp.einsum(form, left, right, precision=PRECISION, preferred_element_type=jnp.float32)


def convolve(imp, panel):
    form = "rk,ks->rs"
    out_re = product(imp[0], panel[0], form) - product(imp[1], panel[1], form)
    out_im = product(imp[0], panel[1], form) + product(imp[1], panel[0], form)
    return jnp.stack([out_re, out_im])


def correlate(res, panel, scale):
    form = "rs,ks->rk"
    out_re = product(res[0], panel[0], form) + product(res[1], panel[1], form)
    out_im = product(res[1], panel[0], form) - product(res[0], panel[1], form)
    return jnp.stack([out_re, out_im]) * scale


def spread_kernel(planes, panel_ref, gath_ref, line_recv, y_recv, send_src, send_up, send_down, send_y, local_sem):
    j = lax.axis_index("shot")
    b = lax.axis_index("rcv")
    z, y = b // 2, lax.rem(b, 2)
    other = z * 2 + 1 - y
    rows, shots = panel_ref.shape[1], panel_ref.shape[2]

    barrier = pltpu.get_barrier_semaphore()
    for d in range(1, planes):
        pl.semaphore_signal(barrier, inc=1, device_id=(lax.rem(j + d, planes), b), device_id_type=MESH)
    pl.semaphore_signal(barrier, inc=1, device_id=(j, other), device_id_type=MESH)

    @pl.when(z < planes - 1)
    def _():
        pl.semaphore_signal(barrier, inc=1, device_id=(j, b + 2), device_id_type=MESH)

    @pl.when(z > 0)
    def _():
        pl.semaphore_signal(barrier, inc=1, device_id=(j, b - 2), device_id_type=MESH)

    ends = (z == 0).astype(jnp.int32) + (z == planes - 1).astype(jnp.int32)
    pl.semaphore_wait(barrier, planes + 2 - ends)

    def slot(a, side, p):
        return gath_ref.at[p, pl.ds(pl.multiple_of(side * rows, rows), rows), pl.ds(pl.multiple_of(a * shots, shots), shots)]

    def source(p):
        i = lax.rem(j - z + planes, planes)
        return pltpu.make_async_remote_copy(
            src_ref=panel_ref.at[p], dst_ref=slot(j, y, p), send_sem=send_src.at[p],
            recv_sem=line_recv.at[i * 2 + p], device_id=(z, b), device_id_type=MESH)

    def own(p):
        return pltpu.make_async_copy(panel_ref.at[p], slot(j, y, p), local_sem.at[p])

    @pl.when(j != z)
    def _():
        for p in range(2):
            source(p).start()

    @pl.when(j == z)
    def _():
        for p in range(2):
            own(p).start()

    def step(i, p):
        a = lax.rem(j + i, planes)
        ref = slot(a, y, p)
        n = i * 2 + p

        def to(dev, send, recv):
            return pltpu.make_async_remote_copy(
                src_ref=ref, dst_ref=ref, send_sem=send.at[n], recv_sem=recv.at[n],
                device_id=(j, dev), device_id_type=MESH)

        return n, to

    up_ok = jnp.logical_and(z >= j, z < planes - 1)
    down_ok = jnp.logical_and(z <= j, z > 0)
    for i in range(planes):
        for p in range(2):
            n, to = step(i, p)
            if i == 0:
                @pl.when(j == z)
                def _():
                    own(p).wait()

                @pl.when(j != z)
                def _():
                    to(other, send_y, line_recv).wait_recv()
            else:
                to(other, send_y, line_recv).wait_recv()

            @pl.when(up_ok)
            def _():
                to(b + 2, send_up, line_recv).start()

            @pl.when(down_ok)
            def _():
                to(b - 2, send_down, line_recv).start()

            to(other, send_y, y_recv).start()

    for i in range(planes):
        for p in range(2):
            n, to = step(i, p)

            @pl.when(up_ok)
            def _():
                to(b + 2, send_up, line_recv).wait_send()

            @pl.when(down_ok)
            def _():
                to(b - 2, send_down, line_recv).wait_send()

            to(other, send_y, y_recv).wait_send()
            a = lax.rem(j + i, planes)
            ref = slot(a, 1 - y, p)
            pltpu.make_async_remote_copy(
                src_ref=ref, dst_ref=ref, send_sem=send_y.at[n], recv_sem=y_recv.at[n],
                device_id=(j, other), device_id_type=MESH).wait_recv()

    @pl.when(j != z)
    def _():
        for p in range(2):
            source(p).wait_send()


def spread(panel, planes):
    _, rows, shots = panel.shape
    dma = pltpu.SemaphoreType.DMA
    return pl.pallas_call(
        functools.partial(spread_kernel, planes),
        out_shape=jax.ShapeDtypeStruct((2, 2 * rows, planes * shots), jnp.float32),
        in_specs=[pl.BlockSpec(memory_space=pl.ANY)],
        out_specs=pl.BlockSpec(memory_space=pl.ANY),
        scratch_shapes=[dma((2 * planes,)), dma((2 * planes,)), dma((2,)), dma((2 * planes,)),
                        dma((2 * planes,)), dma((2 * planes,)), dma((2,))],
        compiler_params=pltpu.CompilerParams(collective_id=0, has_side_effects=True),
    )(panel)


def local(data, impulse, wavelet, live):
    rows_dev = data.shape[2]
    shots_dev = data.shape[3]
    positions = impulse.shape[3]
    groups = lax.axis_size("shot")
    total_shots = shots_dev * groups
    spacing = positions // total_shots
    scale = -(total_shots ** (-0.5))
    j = lax.axis_index("shot")
    mask = live.astype(jnp.float32)
    observed = data[0] * mask[None]
    row_ids = lax.axis_index("rcv") * rows_dev + lax.broadcasted_iota(jnp.int32, (rows_dev, shots_dev), 0)
    col_ids = j * shots_dev + lax.broadcasted_iota(jnp.int32, (rows_dev, shots_dev), 1)
    source = (row_ids == col_ids * spacing).astype(jnp.float32)
    panel = wavelet[0][:, None, None] * source[None] - observed
    if lax.axis_size("rcv") == 2 * groups:
        part = spread(panel, groups)
    else:
        whole = lax.all_gather(panel, "rcv", axis=1, tiled=True)
        part = lax.all_to_all(whole, "shot", split_axis=1, concat_axis=2, tiled=True)
    quarter = positions // groups
    imp = lax.dynamic_slice_in_dim(impulse[0], j * quarter, quarter, axis=2)
    if groups == 4:
        def swap(value, bit):
            return lax.ppermute(value, "shot", [(i, i ^ bit) for i in range(groups)])

        def block(who):
            return lax.dynamic_slice_in_dim(part, who * shots_dev, shots_dev, axis=2)

        def half(chip):
            return lax.dynamic_slice_in_dim(part, chip * 2 * shots_dev, 2 * shots_dev, axis=2)

        def pair(mine, theirs):
            first = j % 2 == 0
            return jnp.concatenate([jnp.where(first, mine, theirs), jnp.where(first, theirs, mine)], axis=2)

        across = convolve(imp, block(j ^ 2)) + swap(convolve(imp, block(j ^ 3)), 1)
        across, imp = lax.optimization_barrier((across, imp))
        far_sum = swap(across, 2)
        near_sum = swap(convolve(imp, block(j ^ 1)), 1)
        predicted = convolve(imp, block(j)) + near_sum + far_sum
        residual = mask[None] * (observed - predicted)
        near = swap(residual, 1)
        far = swap(residual, 2)
        gradient = correlate(pair(residual, near), half(j // 2), scale)
        gradient, far = lax.optimization_barrier((gradient, far))
        corner = swap(far, 1)
        gradient = gradient + correlate(pair(far, corner), half(1 - j // 2), scale)
    else:
        predicted = lax.psum_scatter(convolve(imp, part), "shot", scatter_dimension=2, tiled=True)
        residual = mask[None] * (observed - predicted)
        every = lax.all_gather(residual, "shot", axis=2, tiled=True)
        gradient = correlate(every, part, scale)
    return (residual[None], gradient[None])


def solution(mesh):
    placed = (P(None, None, "rcv", "shot"), P(None, None, "rcv", None), P(), P("rcv", "shot"))
    return jax.shard_map(
        local,
        mesh=mesh,
        in_specs=placed,
        out_specs=(P(None, None, "rcv", "shot"), P(None, None, "rcv", "shot")),
        check_vma=False,
    )
```
